1024 devices in a mesh: fin: 8 (over y, core), fout: 128 (over x, z).
Axes of the slice: x: 4, y: 4, z: 32, core: 2. Of those that a mesh axis runs over, the one named last changes fastest.
Arguments:
- gate_pre: bfloat16 [128, 27648], P('fout', 'fin'), may hold values from -6 to 6
- up_pre: bfloat16 [128, 27648], P('fout', 'fin'), may hold values from -6 to 6
- out_grad: bfloat16 [128, 16384], P(None, 'fout'), may hold values from -12 to 12
- down_weight: bfloat16 [27648, 16384], P('fin', 'fout'), may hold values from -0.0390625 to 0.0390625
Outputs:
- gate_grad: bfloat16 [128, 27648], P('fout', 'fin')
- up_grad: bfloat16 [128, 27648], P('fout', 'fin')
- down_grad: bfloat16 [27648, 16384], P('fin', 'fout')
The draws below stay inside these ranges and needn't reach their ends.
All inputs are finite; a program needn't handle non-finite values.
Results may differ from the reference program's by a relative error of at most 0.0049.
Values may be sent and summed in bfloat16 or wider, within the bound.
A program may use at most 32 MiB of HBM per device.

```python
import jax
import jax.numpy as jnp

FF = 27648
DW = 16384
TOKENS = 128


def with_spikes(values, key, source, target, shards_of, factor):
    owner, partner = [(jnp.arange(values.shape[position]) // (values.shape[position] // shards_of)).reshape([-1 if axis == position else 1 for axis in range(values.ndim)]) for position in (source, target)]
    chosen = jax.random.permutation(key, shards_of)[partner]
    strong = (owner == chosen) | (owner == (partner + shards_of // 2) % shards_of)
    return jnp.where(strong, factor * values, values)


def block_levels(rng, shape, pieces, low, top_value):
    def one(dim, blocks):
        steps = jax.random.uniform(jax.random.fold_in(jax.random.fold_in(rng, 6), dim), (blocks,), jnp.float32, low / len(pieces), top_value / len(pieces))
        return jnp.repeat(jnp.exp(steps), shape[dim] // blocks).reshape((-1,) + (1,) * (len(shape) - dim - 1))

    level = one(*pieces[0])
    for cut in pieces[1:]:
        level = level * one(*cut)
    return level


def normal_values(own_key, dims, deviation, limit, split=(), dtype=jnp.bfloat16):
    values = deviation * jax.random.normal(own_key, dims, jnp.float32)
    if split:
        values = values * block_levels(own_key, dims, split, -0.22, 0.18)
    return jnp.clip(values, -limit, limit).astype(dtype)


def heavy_noise(rng, shape, width, limit, shards, heavy, dtype=jnp.bfloat16):
    entries = width * jax.random.normal(rng, shape, jnp.float32)
    if shards:
        entries = entries * block_levels(rng, shape, shards, -0.22, 0.18)
    return jnp.clip(with_spikes(entries, jax.random.fold_in(rng, 3), *heavy), -limit, limit).astype(dtype)


def setup_inputs(seed: int = 0) -> dict:
    key_list = jax.random.split(jax.random.key(seed), 5)
    gate_pre = normal_values(key_list[0], (TOKENS, FF), 1.0, 6.0, ((0, 128), (1, 8)))
    up_pre = normal_values(key_list[1], (TOKENS, FF), 1.0, 6.0, ((0, 128), (1, 8)))
    out_grad = heavy_noise(key_list[2], (TOKENS, DW), 0.5, 12.0, ((1, 128),), (1, 0, 128, 5.5))
    down_weight = normal_values(key_list[3], (FF, DW), FF ** -0.5, 0.0390625, ((0, 8), (1, 128)))
    return dict(gate_pre=gate_pre, up_pre=up_pre, out_grad=out_grad, down_weight=down_weight)


def reference(gate_pre, up_pre, out_grad, down_weight):
    hidden_grad = jnp.dot(out_grad, down_weight.T, preferred_element_type=jnp.float32)
    gate_float = gate_pre.astype(jnp.float32)
    up_float = up_pre.astype(jnp.float32)
    logistic = jax.nn.sigmoid(gate_float)
    activated = gate_float * logistic
    hidden = (activated * up_float).astype(jnp.bfloat16)
    up_grad = (hidden_grad * activated).astype(jnp.bfloat16)
    gate_grad = (hidden_grad * up_float * logistic * (1.0 + gate_float * (1.0 - logistic))).astype(jnp.bfloat16)
    down_grad = jnp.dot(hidden.T, out_grad, preferred_element_type=jnp.float32).astype(jnp.bfloat16)
    return gate_grad, up_grad, down_grad
```

```python
import jax
import jax.numpy as jnp
from jax import lax
from jax.experimental import pallas as pl
from jax.experimental.pallas import tpu as pltpu
from jax.sharding import PartitionSpec as P

MESH = pl.DeviceIdType.MESH
F32, BF16 = jnp.float32, jnp.bfloat16
NX, NZ = 4, 32
TOK = 128
UNITS = 3456
LANES = 128
CHUNKS = UNITS // LANES
ROWS = 32
HALF = 16


def slot(b, h, k, j=0):
    return (((b * 2 + h) * 4 + k) * 4 + j) * ROWS


def kernel(
    g_ref, u_ref, og_ref, w_ref, gg_ref, ug_ref, dg_ref,
    ogp, part, psend, xrecv, spread, zsend, brecv, asend, arecv, gs, us, outs, held, held32,
    x_send, x_recv, b_send, b_recv, a_send, a_recv,
    ga_send, ga_recv, gb_send, gb_recv, gx_send, gx_recv,
):
    f = lax.axis_index("fout")
    x, z = f // NZ, lax.rem(f, NZ)
    group, cls = z // 4, lax.rem(z, 4)

    def at(dx, dz):
        return {"fout": lax.rem(x + dx + NX, NX) * NZ + lax.rem(z + dz + NZ, NZ)}

    def copy(src, dst, send, recv, device):
        return pltpu.make_async_remote_copy(
            src_ref=src, dst_ref=dst, send_sem=send, recv_sem=recv,
            device_id=device, device_id_type=MESH,
        )

    barrier = pltpu.get_barrier_semaphore()
    peers = [(d, 0) for d in (1, 2, 3)] + [(0, d) for d in (1, -1, 2, -2, 4, -4, 8, -8, 12, -12, 16)]
    for dx, dz in peers:
        pl.semaphore_signal(barrier, inc=1, device_id=at(dx, dz), device_id_type=MESH)

    gs[...] = jnp.zeros_like(gs)
    us[...] = jnp.zeros_like(us)
    for c in range(CHUNKS):
        cols = slice(c * LANES, (c + 1) * LANES)
        gs[c : c + 1, :] = g_ref[:, cols].astype(F32)
        us[c : c + 1, :] = u_ref[:, cols].astype(F32)
    gate, up = gs[...], us[...]
    logistic = 1.0 / (1.0 + jnp.exp(-gate))
    activated = gate * logistic
    mine = pl.multiple_of(group * ROWS + (group // 4) * (12 * ROWS), ROWS)
    held[pl.ds(mine, ROWS), :] = (activated * up).astype(BF16)

    row = lax.broadcasted_iota(jnp.int32, (TOK, TOK), 0)
    token = (
        32 * lax.rem(row // 32 + x, NX)
        + 16 * lax.rem(row // 16, 2)
        + lax.rem(lax.rem(row // 4, 4) + cls, 4)
        + 4 * lax.rem(row, 4)
    )
    pick = (lax.broadcasted_iota(jnp.int32, (TOK, TOK), 1) == token).astype(F32).astype(BF16)
    ogp[...] = jnp.dot(pick, og_ref[...], preferred_element_type=F32).astype(BF16)

    for c in range(CHUNKS):
        cols = slice(c * LANES, (c + 1) * LANES)
        product = lax.dot_general(
            ogp[...], w_ref[cols, :], (((1,), (1,)), ((), ())), preferred_element_type=F32
        )
        part[:, cols] = product[0:32, :]
        psend[:, cols] = product[32:, :].astype(BF16)

    pl.semaphore_wait(barrier, len(peers))

    def x_copy(d, h):
        rows = pl.ds((d - 1) * 32 + h * HALF, HALF)
        return copy(psend.at[rows], xrecv.at[rows], x_send.at[d - 1, h], x_recv.at[d - 1, h], at(d, 0))

    def b_copy(h, k):
        dz = {1: 1, 3: -1, 2: 2 if h == 0 else -2}[k]
        rows = pl.ds(slot(0, h, k), 4 * ROWS)
        return copy(zsend.at[rows], brecv.at[rows], b_send.at[h, k], b_recv.at[h, k], at(0, dz))

    def a_copy(h, j):
        src = asend.at[pl.ds((h * 4 + j) * ROWS, ROWS)]
        dst = arecv.at[pl.ds(pl.multiple_of(group * ROWS, ROWS), ROWS)]
        target = {"fout": x * NZ + 16 * h + 4 * j + cls}
        return copy(src, dst, a_send.at[h * 4 + j], a_recv.at[group], target)

    def ga_copy(j):
        rows = pl.ds(mine, ROWS)
        target = {"fout": x * NZ + 4 * j + cls}
        return copy(held.at[rows], held.at[rows], ga_send.at[j], ga_recv.at[group], target)

    def ga_wait(j):
        rows = pl.ds(slot(0, j // 4, 0, j % 4), ROWS)
        return copy(held.at[rows], held.at[rows], ga_send.at[j], ga_recv.at[j], at(0, 1))

    def gb_copy(h, k):
        dz = {1: -1, 3: 1, 2: 2 if h == 0 else -2}[k]
        src, dst = pl.ds(slot(0, h, 0), 4 * ROWS), pl.ds(slot(0, h, k), 4 * ROWS)
        return copy(held.at[src], held.at[dst], gb_send.at[h, k], gb_recv.at[h, k], at(0, dz))

    def gx_copy(b, h, k):
        src, dst = pl.ds(slot(0, h, k), 4 * ROWS), pl.ds(slot(b, h, k), 4 * ROWS)
        return copy(held.at[src], held.at[dst], gx_send.at[b, h, k], gx_recv.at[b, h, k], at(-b, 0))

    def unpack(b, h, k):
        rows = pl.ds(slot(b, h, k), 4 * ROWS)
        held32[rows, :] = held[rows, :].astype(F32)

    def start_x():
        for h in (0, 1):
            for d in (2, 1, 3):
                x_copy(d, h).start()

    def start_gather():
        for j in range(8):
            @pl.when(group != j)
            def _():
                ga_copy(j).start()

    def sum_x(h):
        for d in (1, 3, 2):
            x_copy(d, h).wait_recv()
        for c in range(CHUNKS):
            cols = slice(c * LANES, (c + 1) * LANES)
            total = part[h * HALF : (h + 1) * HALF, cols]
            for d in (1, 2, 3):
                start = (d - 1) * 32 + h * HALF
                total += xrecv[start : start + HALF, cols].astype(F32)
            spread[pl.ds(h * HALF * ROWS + c, HALF, stride=ROWS), :] = total
        first = slot(0, h, 1)
        rows = pl.ds(first, 12 * ROWS)
        zsend[rows, :] = spread[rows, :].astype(BF16)
        for k in (2, 1, 3):
            b_copy(h, k).start()

    def sum_b(h):
        for k in (1, 3, 2):
            b_copy(h, k).wait_recv()
        total = spread[pl.ds(slot(0, h, 0), 4 * ROWS), :]
        for k in (1, 2, 3):
            total += brecv[pl.ds(slot(0, h, k), 4 * ROWS), :].astype(F32)
        asend[pl.ds(h * 4 * ROWS, 4 * ROWS), :] = total.astype(BF16)
        for j in range(4):
            @pl.when(group != h * 4 + j)
            def _():
                a_copy(h, j).start()

            @pl.when(group == h * 4 + j)
            def _():
                arecv[pl.ds((h * 4 + j) * ROWS, ROWS), :] = asend[pl.ds((h * 4 + j) * ROWS, ROWS), :]

    def gather_a(h):
        for j in range(4 * h, 4 * h + 4):
            @pl.when(group != j)
            def _():
                ga_wait(j).wait_recv()
        for k in (2, 1, 3):
            gb_copy(h, k).start()
        for b in (2, 1, 3):
            gx_copy(b, h, 0).start()
        unpack(0, h, 0)

    def gather_b(h, k):
        gb_copy(h, k).wait_recv()
        for b in (2, 1, 3):
            gx_copy(b, h, k).start()
        unpack(0, h, k)

    def finish_sums():
        for j in range(8):
            @pl.when(group != j)
            def _():
                rows = pl.ds(j * ROWS, ROWS)
                copy(asend.at[rows], arecv.at[rows], a_send.at[j], a_recv.at[j], at(0, 1)).wait_recv()
        upstream = arecv[0:ROWS, :].astype(F32)
        for j in range(1, 8):
            upstream += arecv[j * ROWS : (j + 1) * ROWS, :].astype(F32)
        gate, up = gs[...], us[...]
        logistic = 1.0 / (1.0 + jnp.exp(-gate))
        outs[0:ROWS, :] = upstream * up * logistic * (1.0 + gate * (1.0 - logistic))
        outs[ROWS:, :] = upstream * (gate * logistic)
        for c in range(CHUNKS):
            cols = slice(c * LANES, (c + 1) * LANES)
            gg_ref[:, cols] = outs[c : c + 1, :].astype(BF16)
            ug_ref[:, cols] = outs[ROWS + c : ROWS + c + 1, :].astype(BF16)

    start_gather()
    start_x()
    sum_x(0)
    sum_x(1)
    sum_b(0)
    sum_b(1)
    gather_a(0)
    gather_a(1)
    for h in (0, 1):
        for k in (1, 3, 2):
            gather_b(h, k)
    finish_sums()
    for b in (1, 3, 2):
        for h in (0, 1):
            for k in range(4):
                gx_copy(b, h, k).wait_recv()
                unpack(b, h, k)

    for c in range(CHUNKS):
        hidden = held32[pl.ds(c, TOK, stride=ROWS), :].astype(BF16)
        grad = lax.dot_general(
            hidden, ogp[...], (((0,), (0,)), ((), ())), preferred_element_type=F32
        )
        dg_ref[c * LANES : (c + 1) * LANES, :] = grad.astype(BF16)

    for h in (0, 1):
        for d in (1, 2, 3):
            x_copy(d, h).wait_send()
        for k in (1, 2, 3):
            b_copy(h, k).wait_send()
            gb_copy(h, k).wait_send()
        for j in range(4):
            @pl.when(group != h * 4 + j)
            def _():
                a_copy(h, j).wait_send()
                ga_copy(h * 4 + j).wait_send()
        for b in (1, 2, 3):
            for k in range(4):
                gx_copy(b, h, k).wait_send()


def local(gate_pre, up_pre, out_grad, down_weight):
    dma = pltpu.SemaphoreType.DMA
    vmem = pl.BlockSpec(memory_space=pltpu.VMEM)
    return pl.pallas_call(
        kernel,
        out_shape=(
            jax.ShapeDtypeStruct((1, UNITS), BF16),
            jax.ShapeDtypeStruct((1, UNITS), BF16),
            jax.ShapeDtypeStruct((UNITS, LANES), BF16),
        ),
        in_specs=[vmem] * 4,
        out_specs=(vmem,) * 3,
        scratch_shapes=[
            pltpu.VMEM((TOK, LANES), BF16),
            pltpu.VMEM((32, UNITS), F32),
            pltpu.VMEM((96, UNITS), BF16),
            pltpu.VMEM((96, UNITS), BF16),
            pltpu.VMEM((32 * ROWS, LANES), F32),
            pltpu.VMEM((32 * ROWS, LANES), BF16),
            pltpu.VMEM((32 * ROWS, LANES), BF16),
            pltpu.VMEM((8 * ROWS, LANES), BF16),
            pltpu.VMEM((8 * ROWS, LANES), BF16),
            pltpu.VMEM((ROWS, LANES), F32),
            pltpu.VMEM((ROWS, LANES), F32),
            pltpu.VMEM((2 * ROWS, LANES), F32),
            pltpu.VMEM((TOK * ROWS, LANES), BF16),
            pltpu.VMEM((TOK * ROWS, LANES), F32),
            dma((3, 2)), dma((3, 2)),
            dma((2, 4)), dma((2, 4)),
            dma((8,)), dma((8,)),
            dma((8,)), dma((8,)),
            dma((2, 4)), dma((2, 4)),
            dma((4, 2, 4)), dma((4, 2, 4)),
        ],
        compiler_params=pltpu.CompilerParams(
            collective_id=0, has_side_effects=True, vmem_limit_bytes=40 * 2**20
        ),
    )(gate_pre, up_pre, out_grad, down_weight)


def solution(mesh):
    placed = (P("fout", "fin"), P("fout", "fin"), P(None, "fout"), P("fin", "fout"))
    return jax.shard_map(
        local,
        mesh=mesh,
        in_specs=placed,
        out_specs=(P("fout", "fin"), P("fout", "fin"), P("fin", "fout")),
        check_vma=False,
    )
```

```python
import jax
import jax.numpy as jnp
from jax import lax
from jax.experimental import pallas as pl
from jax.experimental.pallas import tpu as pltpu
from jax.sharding import PartitionSpec as P

MESH = pl.DeviceIdType.MESH
F32, BF16 = jnp.float32, jnp.bfloat16
NX, NZ = 4, 32
TOK = 128
UNITS = 3456
LANES = 128
CHUNKS = UNITS // LANES
ROWS = 32
HALF = 16
GROUPS = NZ // 4


def slot(b, h, k, j=0):
    return (((b * 2 + h) * 4 + k) * 4 + j) * ROWS


def kernel(
    g_hbm, u_hbm, og_hbm, w_hbm, gg_ref, ug_ref, dg_ref,
    g_ref, u_ref, og_ref, w_ref,
    ogp, part, psend, xrecv, spread, zsend, brecv, asend, arecv, gs, us, outs, held, held32,
    in_sem, x_send, x_recv, b_send, b_recv, a_send, a_recv,
    ga_send, ga_recv, gb_send, gb_recv, gx_send, gx_recv,
):
    f = lax.axis_index("fout")
    x, z = f // NZ, lax.rem(f, NZ)
    group, cls = z // 4, lax.rem(z, 4)

    def at(dx, dz):
        return {"fout": lax.rem(x + dx + NX, NX) * NZ + lax.rem(z + dz + NZ, NZ)}

    def copy(src, dst, send, recv, device):
        return pltpu.make_async_remote_copy(
            src_ref=src, dst_ref=dst, send_sem=send, recv_sem=recv,
            device_id=device, device_id_type=MESH,
        )

    def signal(sem, device):
        pl.semaphore_signal(sem, inc=1, device_id=device, device_id_type=MESH)

    def beside(k):
        return at(0, lax.rem(cls + k, 4) - cls)

    barrier = pltpu.get_barrier_semaphore()
    for d in (1, 2, 3):
        signal(barrier, beside(d))
    for d in (1, 2, 3):
        signal(barrier, at(d, 0))
    for m in range(1, GROUPS):
        @pl.when(group + m < GROUPS)
        def _():
            signal(barrier, at(0, 4 * m))

    fetch = [
        pltpu.make_async_copy(src, dst, in_sem.at[i])
        for i, (src, dst) in enumerate(((w_hbm, w_ref), (og_hbm, og_ref), (g_hbm, g_ref), (u_hbm, u_ref)))
    ]
    for c in fetch:
        c.start()

    row = lax.broadcasted_iota(jnp.int32, (TOK, TOK), 0)
    token = (
        32 * lax.rem(row // 32 + x, NX)
        + 16 * lax.rem(row // 16, 2)
        + lax.rem(lax.rem(row // 4, 4) + cls, 4)
        + 4 * lax.rem(row, 4)
    )
    pick = (lax.broadcasted_iota(jnp.int32, (TOK, TOK), 1) == token).astype(F32).astype(BF16)

    gs[...] = jnp.zeros_like(gs)
    us[...] = jnp.zeros_like(us)
    fetch[2].wait()
    fetch[3].wait()
    for c in range(CHUNKS):
        cols = slice(c * LANES, (c + 1) * LANES)
        gs[c : c + 1, :] = g_ref[:, cols].astype(F32)
        us[c : c + 1, :] = u_ref[:, cols].astype(F32)
    gate, up = gs[...], us[...]
    logistic = 1.0 / (1.0 + jnp.exp(-gate))
    activated = gate * logistic
    mine = pl.multiple_of(group * ROWS + (group // 4) * (12 * ROWS), ROWS)
    held[pl.ds(mine, ROWS), :] = (activated * up).astype(BF16)

    fetch[1].wait()
    ogp[...] = jnp.dot(pick, og_ref[...], preferred_element_type=F32).astype(BF16)

    fetch[0].wait()
    for c in range(CHUNKS):
        cols = slice(c * LANES, (c + 1) * LANES)
        product = lax.dot_general(
            ogp[...], w_ref[cols, :], (((1,), (1,)), ((), ())), preferred_element_type=F32
        )
        part[:, cols] = product[0:32, :]
        psend[:, cols] = product[32:, :].astype(BF16)

    pl.semaphore_wait(barrier, 6 + group)

    def x_copy(d, h):
        rows = pl.ds((d - 1) * 32 + h * HALF, HALF)
        return copy(psend.at[rows], xrecv.at[rows], x_send.at[d - 1, h], x_recv.at[d - 1, h], at(d, 0))

    def b_copy(h, k):
        rows = pl.ds(slot(0, h, k), 4 * ROWS)
        return copy(zsend.at[rows], brecv.at[rows], b_send.at[h, k], b_recv.at[h, k], beside(k))

    def a_copy(h, j):
        src = asend.at[pl.ds((h * 4 + j) * ROWS, ROWS)]
        dst = arecv.at[pl.ds(pl.multiple_of(group * ROWS, ROWS), ROWS)]
        target = {"fout": x * NZ + 16 * h + 4 * j + cls}
        return copy(src, dst, a_send.at[h * 4 + j], a_recv.at[group], target)

    def ga_copy(j):
        rows = pl.ds(mine, ROWS)
        target = {"fout": x * NZ + 4 * j + cls}
        return copy(held.at[rows], held.at[rows], ga_send.at[j], ga_recv.at[group], target)

    def ga_wait(j):
        rows = pl.ds(slot(0, j // 4, 0, j % 4), ROWS)
        return copy(held.at[rows], held.at[rows], ga_send.at[j], ga_recv.at[j], at(0, 1))

    def gb_copy(h, k):
        src, dst = pl.ds(slot(0, h, 0), 4 * ROWS), pl.ds(slot(0, h, k), 4 * ROWS)
        return copy(held.at[src], held.at[dst], gb_send.at[h, k], gb_recv.at[h, k], beside(4 - k))

    def gx_copy(b, h, k):
        src, dst = pl.ds(slot(0, h, k), 4 * ROWS), pl.ds(slot(b, h, k), 4 * ROWS)
        return copy(held.at[src], held.at[dst], gx_send.at[b, h, k], gx_recv.at[b, h, k], at(-b, 0))

    def unpack(b, h, k):
        rows = pl.ds(slot(b, h, k), 4 * ROWS)
        held32[rows, :] = held[rows, :].astype(F32)

    def sum_x(h):
        for d in (1, 3, 2):
            x_copy(d, h).wait_recv()
        for c in range(CHUNKS):
            cols = slice(c * LANES, (c + 1) * LANES)
            total = part[h * HALF : (h + 1) * HALF, cols]
            for d in (1, 2, 3):
                start = (d - 1) * 32 + h * HALF
                total += xrecv[start : start + HALF, cols].astype(F32)
            spread[pl.ds(h * HALF * ROWS + c, HALF, stride=ROWS), :] = total
        rows = pl.ds(slot(0, h, 1), 12 * ROWS)
        zsend[rows, :] = spread[rows, :].astype(BF16)
        for k in (2, 1, 3):
            b_copy(h, k).start()

    def sum_b(h):
        for k in (1, 3, 2):
            b_copy(h, k).wait_recv()
        total = spread[pl.ds(slot(0, h, 0), 4 * ROWS), :]
        for k in (1, 2, 3):
            total += brecv[pl.ds(slot(0, h, k), 4 * ROWS), :].astype(F32)
        asend[pl.ds(h * 4 * ROWS, 4 * ROWS), :] = total.astype(BF16)
        for j in range(4):
            @pl.when(group > h * 4 + j)
            def _():
                a_copy(h, j).start()

            @pl.when(group == h * 4 + j)
            def _():
                arecv[pl.ds((h * 4 + j) * ROWS, ROWS), :] = asend[pl.ds((h * 4 + j) * ROWS, ROWS), :]

    def above(h):
        for j in range(4 * h, 4 * h + 4):
            @pl.when(group < j)
            def _():
                ga_wait(j).wait_recv()
                ga_copy(j).start()
                a_copy(h, j - 4 * h).start()

    def below(h):
        for j in range(4 * h, 4 * h + 4):
            @pl.when(group > j)
            def _():
                ga_wait(j).wait_recv()

    def gather_a(h):
        for k in (2, 1, 3):
            gb_copy(h, k).start()
        for b in (2, 1, 3):
            gx_copy(b, h, 0).start()
        unpack(0, h, 0)

    def gather_b(h):
        for k in (1, 3, 2):
            gb_copy(h, k).wait_recv()
            for b in (2, 1, 3):
                gx_copy(b, h, k).start()
            unpack(0, h, k)

    def finish_sums():
        for j in range(8):
            @pl.when(group != j)
            def _():
                rows = pl.ds(j * ROWS, ROWS)
                copy(asend.at[rows], arecv.at[rows], a_send.at[j], a_recv.at[j], at(0, 1)).wait_recv()
        upstream = arecv[0:ROWS, :].astype(F32)
        for j in range(1, 8):
            upstream += arecv[j * ROWS : (j + 1) * ROWS, :].astype(F32)
        gate, up = gs[...], us[...]
        logistic = 1.0 / (1.0 + jnp.exp(-gate))
        outs[0:ROWS, :] = upstream * up * logistic * (1.0 + gate * (1.0 - logistic))
        outs[ROWS:, :] = upstream * (gate * logistic)
        for c in range(CHUNKS):
            cols = slice(c * LANES, (c + 1) * LANES)
            gg_ref[:, cols] = outs[c : c + 1, :].astype(BF16)
            ug_ref[:, cols] = outs[ROWS + c : ROWS + c + 1, :].astype(BF16)

    for j in range(GROUPS - 1):
        @pl.when(group > j)
        def _():
            ga_copy(j).start()
    for d in (2, 1, 3):
        x_copy(d, 0).start()
    for d in (2, 1, 3):
        x_copy(d, 0).wait_send()
    for d in (2, 1, 3):
        x_copy(d, 1).start()
    for h in (0, 1):
        sum_x(h)
        sum_b(h)

    @pl.when(group < 3)
    def _():
        above(0)
        below(0)
        gather_a(0)
        gather_b(0)
        above(1)
        gather_a(1)
        gather_b(1)

    @pl.when(group >= 3)
    def _():
        above(1)
        below(1)
        gather_a(1)
        gather_b(1)
        below(0)
        gather_a(0)
        gather_b(0)

    finish_sums()
    for b in (1, 3, 2):
        for h in (0, 1):
            for k in range(4):
                gx_copy(b, h, k).wait_recv()
                unpack(b, h, k)

    for c in range(CHUNKS):
        hidden = held32[pl.ds(c, TOK, stride=ROWS), :].astype(BF16)
        grad = lax.dot_general(
            hidden, ogp[...], (((0,), (0,)), ((), ())), preferred_element_type=F32
        )
        dg_ref[c * LANES : (c + 1) * LANES, :] = grad.astype(BF16)

    for h in (0, 1):
        if h == 1:
            for d in (1, 2, 3):
                x_copy(d, h).wait_send()
        for k in (1, 2, 3):
            b_copy(h, k).wait_send()
            gb_copy(h, k).wait_send()
        for j in range(4):
            @pl.when(group != h * 4 + j)
            def _():
                a_copy(h, j).wait_send()
        for b in (1, 2, 3):
            for k in range(4):
                gx_copy(b, h, k).wait_send()
    for j in range(GROUPS):
        @pl.when(group != j)
        def _():
            ga_copy(j).wait_send()


def local(gate_pre, up_pre, out_grad, down_weight):
    dma = pltpu.SemaphoreType.DMA
    vmem = pl.BlockSpec(memory_space=pltpu.VMEM)
    shapes = (
        jax.ShapeDtypeStruct((1, UNITS), BF16),
        jax.ShapeDtypeStruct((1, UNITS), BF16),
        jax.ShapeDtypeStruct((UNITS, LANES), BF16),
    )
    anywhere = pl.BlockSpec(memory_space=pl.ANY)
    operands = [
        pltpu.with_memory_space_constraint(a, pltpu.HBM)
        for a in (gate_pre, up_pre, out_grad, down_weight)
    ]
    return pl.pallas_call(
        kernel,
        out_shape=shapes,
        in_specs=[anywhere] * 4,
        out_specs=(vmem,) * 3,
        scratch_shapes=[
            pltpu.VMEM((1, UNITS), BF16),
            pltpu.VMEM((1, UNITS), BF16),
            pltpu.VMEM((TOK, LANES), BF16),
            pltpu.VMEM((UNITS, LANES), BF16),
            pltpu.VMEM((TOK, LANES), BF16),
            pltpu.VMEM((32, UNITS), F32),
            pltpu.VMEM((96, UNITS), BF16),
            pltpu.VMEM((96, UNITS), BF16),
            pltpu.VMEM((32 * ROWS, LANES), F32),
            pltpu.VMEM((32 * ROWS, LANES), BF16),
            pltpu.VMEM((32 * ROWS, LANES), BF16),
            pltpu.VMEM((8 * ROWS, LANES), BF16),
            pltpu.VMEM((8 * ROWS, LANES), BF16),
            pltpu.VMEM((ROWS, LANES), F32),
            pltpu.VMEM((ROWS, LANES), F32),
            pltpu.VMEM((2 * ROWS, LANES), F32),
            pltpu.VMEM((TOK * ROWS, LANES), BF16),
            pltpu.VMEM((TOK * ROWS, LANES), F32),
            dma((4,)),
            dma((3, 2)), dma((3, 2)),
            dma((2, 4)), dma((2, 4)),
            dma((8,)), dma((8,)),
            dma((8,)), dma((8,)),
            dma((2, 4)), dma((2, 4)),
            dma((4, 2, 4)), dma((4, 2, 4)),
        ],
        compiler_params=pltpu.CompilerParams(
            collective_id=0, has_side_effects=True, vmem_limit_bytes=32 * 2**20
        ),
    )(*operands)


def solution(mesh):
    placed = (P("fout", "fin"), P("fout", "fin"), P(None, "fout"), P("fin", "fout"))
    return jax.shard_map(
        local,
        mesh=mesh,
        in_specs=placed,
        out_specs=(P("fout", "fin"), P("fout", "fin"), P("fin", "fout")),
        check_vma=False,
    )
```

```python
import jax
import jax.numpy as jnp
from jax import lax
from jax.experimental import pallas as pl
from jax.experimental.pallas import tpu as pltpu
from jax.sharding import PartitionSpec as P

MESH = pl.DeviceIdType.MESH
F32, BF16 = jnp.float32, jnp.bfloat16
NX, NZ = 4, 32
TOK = 128
UNITS = 3456
LANES = 128
CHUNKS = UNITS // LANES
ROWS = 32
HALF = 16
GROUPS = NZ // 4


def slot(b, h, k, j=0):
    return (((b * 2 + h) * 4 + k) * 4 + j) * ROWS


def kernel(
    g_hbm, u_hbm, og_hbm, w_hbm, gg_ref, ug_ref, dg_ref,
    g_ref, u_ref, og_ref, w_ref,
    ogp, part, psend, xrecv, spread, zsend, brecv, asend, arecv, gs, us, outs, held, held32,
    in_sem, x_send, x_recv, b_send, b_recv, a_send, a_recv,
    ga_send, ga_recv, gb_send, gb_recv, gx_send, gx_recv,
):
    f = lax.axis_index("fout")
    x, z = f // NZ, lax.rem(f, NZ)
    group, cls = z // 4, lax.rem(z, 4)

    def at(dx, dz):
        return {"fout": lax.rem(x + dx + NX, NX) * NZ + lax.rem(z + dz + NZ, NZ)}

    def copy(src, dst, send, recv, device):
        return pltpu.make_async_remote_copy(
            src_ref=src, dst_ref=dst, send_sem=send, recv_sem=recv,
            device_id=device, device_id_type=MESH,
        )

    def signal(sem, device):
        pl.semaphore_signal(sem, inc=1, device_id=device, device_id_type=MESH)

    def beside(k):
        return at(0, lax.rem(cls + k, 4) - cls)

    barrier = pltpu.get_barrier_semaphore()
    for d in (1, 2, 3):
        signal(barrier, beside(d))
    for d in (1, 2, 3):
        signal(barrier, at(d, 0))
    for m in range(1, GROUPS):
        @pl.when(group + m < GROUPS)
        def _():
            signal(barrier, at(0, 4 * m))

    fetch = [
        pltpu.make_async_copy(src, dst, in_sem.at[i])
        for i, (src, dst) in enumerate(((w_hbm, w_ref), (og_hbm, og_ref), (g_hbm, g_ref), (u_hbm, u_ref)))
    ]
    for c in fetch:
        c.start()

    row = lax.broadcasted_iota(jnp.int32, (TOK, TOK), 0)
    token = (
        32 * lax.rem(row // 32 + x, NX)
        + 16 * lax.rem(row // 16, 2)
        + lax.rem(lax.rem(row // 4, 4) + cls, 4)
        + 4 * lax.rem(row, 4)
    )
    pick = (lax.broadcasted_iota(jnp.int32, (TOK, TOK), 1) == token).astype(F32).astype(BF16)

    gs[...] = jnp.zeros_like(gs)
    us[...] = jnp.zeros_like(us)
    fetch[2].wait()
    fetch[3].wait()
    for c in range(CHUNKS):
        cols = slice(c * LANES, (c + 1) * LANES)
        gs[c : c + 1, :] = g_ref[:, cols].astype(F32)
        us[c : c + 1, :] = u_ref[:, cols].astype(F32)
    gate, up = gs[...], us[...]
    logistic = 1.0 / (1.0 + jnp.exp(-gate))
    activated = gate * logistic
    mine = pl.multiple_of(group * ROWS + (group // 4) * (12 * ROWS), ROWS)
    held[pl.ds(mine, ROWS), :] = (activated * up).astype(BF16)

    fetch[1].wait()
    ogp[...] = jnp.dot(pick, og_ref[...], preferred_element_type=F32).astype(BF16)

    fetch[0].wait()
    for c in range(CHUNKS):
        cols = slice(c * LANES, (c + 1) * LANES)
        product = lax.dot_general(
            ogp[...], w_ref[cols, :], (((1,), (1,)), ((), ())), preferred_element_type=F32
        )
        part[:, cols] = product[0:32, :]
        psend[:, cols] = product[32:, :].astype(BF16)

    pl.semaphore_wait(barrier, 6 + group)

    def x_copy(d, h):
        rows = pl.ds((d - 1) * 32 + h * HALF, HALF)
        return copy(psend.at[rows], xrecv.at[rows], x_send.at[h], x_recv.at[h], at(d, 0))

    def b_copy(h, k):
        rows = pl.ds(slot(0, h, k), 4 * ROWS)
        return copy(zsend.at[rows], brecv.at[rows], b_send.at[h], b_recv.at[h], beside(k))

    def a_copy(h, j):
        src = asend.at[pl.ds((h * 4 + j) * ROWS, ROWS)]
        dst = arecv.at[pl.ds(pl.multiple_of(group * ROWS, ROWS), ROWS)]
        target = {"fout": x * NZ + 16 * h + 4 * j + cls}
        return copy(src, dst, a_send.at[0], a_recv.at[0], target)

    def ga_copy(j):
        rows = pl.ds(mine, ROWS)
        target = {"fout": x * NZ + 4 * j + cls}
        return copy(held.at[rows], held.at[rows], ga_send.at[0], ga_recv.at[group], target)

    def ga_wait(j):
        rows = pl.ds(slot(0, j // 4, 0, j % 4), ROWS)
        return copy(held.at[rows], held.at[rows], ga_send.at[0], ga_recv.at[j], at(1, 0))

    def gb_copy(h, k):
        src, dst = pl.ds(slot(0, h, 0), 4 * ROWS), pl.ds(slot(0, h, k), 4 * ROWS)
        return copy(held.at[src], held.at[dst], gb_send.at[h], gb_recv.at[h], beside(4 - k))

    def gx_copy(b, h, others):
        first, rows = (1, 12 * ROWS) if others else (0, 4 * ROWS)
        src, dst = pl.ds(slot(0, h, first), rows), pl.ds(slot(b, h, first), rows)
        return copy(held.at[src], held.at[dst], gx_send.at[0], gx_recv.at[h, others], at(-b, 0))

    def arrived(ref, rows, sem):
        whole = ref.at[pl.ds(0, rows)]
        copy(whole, whole, sem, sem, at(1, 0)).wait_recv()

    def left(ref, rows, sem):
        whole = ref.at[pl.ds(0, rows)]
        copy(whole, whole, sem, sem, at(1, 0)).wait_send()

    def unpack(b, h, k):
        rows = pl.ds(slot(b, h, k), 4 * ROWS)
        held32[rows, :] = held[rows, :].astype(F32)

    def sum_x(h):
        arrived(xrecv, 3 * HALF, x_recv.at[h])
        for c in range(CHUNKS):
            cols = slice(c * LANES, (c + 1) * LANES)
            total = part[h * HALF : (h + 1) * HALF, cols]
            for d in (1, 2, 3):
                start = (d - 1) * 32 + h * HALF
                total += xrecv[start : start + HALF, cols].astype(F32)
            spread[pl.ds(h * HALF * ROWS + c, HALF, stride=ROWS), :] = total
        rows = pl.ds(slot(0, h, 1), 12 * ROWS)
        zsend[rows, :] = spread[rows, :].astype(BF16)
        for k in (2, 1, 3):
            b_copy(h, k).start()

    def sum_b(h):
        arrived(brecv, 12 * ROWS, b_recv.at[h])
        total = spread[pl.ds(slot(0, h, 0), 4 * ROWS), :]
        for k in (1, 2, 3):
            total += brecv[pl.ds(slot(0, h, k), 4 * ROWS), :].astype(F32)
        asend[pl.ds(h * 4 * ROWS, 4 * ROWS), :] = total.astype(BF16)
        for j in range(4):
            @pl.when(group > h * 4 + j)
            def _():
                a_copy(h, j).start()

            @pl.when(group == h * 4 + j)
            def _():
                arecv[pl.ds((h * 4 + j) * ROWS, ROWS), :] = asend[pl.ds((h * 4 + j) * ROWS, ROWS), :]

    def answer_row(j):
        @pl.when(group < j)
        def _():
            ga_wait(j).wait_recv()
            ga_copy(j).start()

    def answer_sum(j):
        @pl.when(group < j)
        def _():
            a_copy(j // 4, j % 4).start()

    def below(h):
        for j in range(4 * h, 4 * h + 4):
            @pl.when(group > j)
            def _():
                ga_wait(j).wait_recv()

    def gather(h):
        for k in (2, 1, 3):
            gb_copy(h, k).start()
        for b in (2, 1, 3):
            gx_copy(b, h, 0).start()
        unpack(0, h, 0)
        arrived(held, 12 * ROWS, gb_recv.at[h])
        for b in (2, 1, 3):
            gx_copy(b, h, 1).start()
        for k in (1, 2, 3):
            unpack(0, h, k)

    def finish_sums():
        arrived(arecv, 7 * ROWS, a_recv.at[0])
        upstream = arecv[0:ROWS, :].astype(F32)
        for j in range(1, 8):
            upstream += arecv[j * ROWS : (j + 1) * ROWS, :].astype(F32)
        gate, up = gs[...], us[...]
        logistic = 1.0 / (1.0 + jnp.exp(-gate))
        outs[0:ROWS, :] = upstream * up * logistic * (1.0 + gate * (1.0 - logistic))
        outs[ROWS:, :] = upstream * (gate * logistic)
        for c in range(CHUNKS):
            cols = slice(c * LANES, (c + 1) * LANES)
            gg_ref[:, cols] = outs[c : c + 1, :].astype(BF16)
            ug_ref[:, cols] = outs[ROWS + c : ROWS + c + 1, :].astype(BF16)

    for j in range(GROUPS - 1):
        @pl.when(group > j)
        def _():
            ga_copy(j).start()
    for d in (2, 1, 3):
        x_copy(d, 0).start()
    left(psend, 3 * HALF, x_send.at[0])
    for d in (2, 1, 3):
        x_copy(d, 1).start()
    sum_x(0)
    sum_b(0)

    @pl.when(group == 3)
    def _():
        answer_row(4)
        answer_row(5)

    sum_x(1)

    @pl.when(group == 3)
    def _():
        answer_row(6)

    sum_b(1)

    @pl.when(group < 3)
    def _():
        for j in (1, 2, 3):
            answer_row(j)
            answer_sum(j)
        below(0)
        gather(0)
        for j in (4, 5, 6, 7):
            answer_row(j)
            answer_sum(j)
        gather(1)

    @pl.when(group >= 3)
    def _():
        for j in (4, 5, 6):
            @pl.when(group != 3)
            def _():
                answer_row(j)

            answer_sum(j)
        answer_row(7)
        answer_sum(7)
        below(1)
        gather(1)
        below(0)
        gather(0)

    finish_sums()
    for h in (0, 1):
        for others in (0, 1):
            arrived(held, (36 if others else 12) * ROWS, gx_recv.at[h, others])
            for b in (1, 2, 3):
                for k in (1, 2, 3) if others else (0,):
                    unpack(b, h, k)

    for c in range(CHUNKS):
        hidden = held32[pl.ds(c, TOK, stride=ROWS), :].astype(BF16)
        grad = lax.dot_general(
            hidden, ogp[...], (((0,), (0,)), ((), ())), preferred_element_type=F32
        )
        dg_ref[c * LANES : (c + 1) * LANES, :] = grad.astype(BF16)

    left(psend, 3 * HALF, x_send.at[1])
    for h in (0, 1):
        left(zsend, 12 * ROWS, b_send.at[h])
        left(held, 12 * ROWS, gb_send.at[h])
    left(asend, 7 * ROWS, a_send.at[0])
    left(held, 7 * ROWS, ga_send.at[0])
    left(held, 96 * ROWS, gx_send.at[0])


def local(gate_pre, up_pre, out_grad, down_weight):
    dma = pltpu.SemaphoreType.DMA
    vmem = pl.BlockSpec(memory_space=pltpu.VMEM)
    shapes = (
        jax.ShapeDtypeStruct((1, UNITS), BF16),
        jax.ShapeDtypeStruct((1, UNITS), BF16),
        jax.ShapeDtypeStruct((UNITS, LANES), BF16),
    )
    anywhere = pl.BlockSpec(memory_space=pl.ANY)
    operands = [
        pltpu.with_memory_space_constraint(a, pltpu.HBM)
        for a in (gate_pre, up_pre, out_grad, down_weight)
    ]
    return pl.pallas_call(
        kernel,
        out_shape=shapes,
        in_specs=[anywhere] * 4,
        out_specs=(vmem,) * 3,
        scratch_shapes=[
            pltpu.VMEM((1, UNITS), BF16),
            pltpu.VMEM((1, UNITS), BF16),
            pltpu.VMEM((TOK, LANES), BF16),
            pltpu.VMEM((UNITS, LANES), BF16),
            pltpu.VMEM((TOK, LANES), BF16),
            pltpu.VMEM((32, UNITS), F32),
            pltpu.VMEM((96, UNITS), BF16),
            pltpu.VMEM((96, UNITS), BF16),
            pltpu.VMEM((32 * ROWS, LANES), F32),
            pltpu.VMEM((32 * ROWS, LANES), BF16),
            pltpu.VMEM((32 * ROWS, LANES), BF16),
            pltpu.VMEM((8 * ROWS, LANES), BF16),
            pltpu.VMEM((8 * ROWS, LANES), BF16),
            pltpu.VMEM((ROWS, LANES), F32),
            pltpu.VMEM((ROWS, LANES), F32),
            pltpu.VMEM((2 * ROWS, LANES), F32),
            pltpu.VMEM((TOK * ROWS, LANES), BF16),
            pltpu.VMEM((TOK * ROWS, LANES), F32),
            dma((4,)),
            dma((2,)), dma((2,)),
            dma((2,)), dma((2,)),
            dma((1,)), dma((1,)),
            dma((1,)), dma((8,)),
            dma((2,)), dma((2,)),
            dma((1,)), dma((2, 2)),
        ],
        compiler_params=pltpu.CompilerParams(
            collective_id=0, has_side_effects=True, vmem_limit_bytes=32 * 2**20
        ),
    )(*operands)


def solution(mesh):
    placed = (P("fout", "fin"), P("fout", "fin"), P(None, "fout"), P("fin", "fout"))
    return jax.shard_map(
        local,
        mesh=mesh,
        in_specs=placed,
        out_specs=(P("fout", "fin"), P("fout", "fin"), P("fin", "fout")),
        check_vma=False,
    )
```

```python
import jax
import jax.numpy as jnp
from jax import lax
from jax.experimental import pallas as pl
from jax.experimental.pallas import tpu as pltpu
from jax.sharding import PartitionSpec as P

MESH = pl.DeviceIdType.MESH
F32, BF16 = jnp.float32, jnp.bfloat16
NX, NZ = 4, 32
TOK = 128
UNITS = 3456
LANES = 128
CHUNKS = UNITS // LANES
ROWS = 32
HALF = 16
GROUPS = NZ // 4


def slot(b, h, k, j=0):
    return (((b * 2 + h) * 4 + k) * 4 + j) * ROWS


def kernel(
    g_hbm, u_hbm, og_hbm, w_hbm, gg_ref, ug_ref, dg_ref,
    g_ref, u_ref, og_ref, w_ref,
    ogp, part, psend, xrecv, spread, zsend, brecv, asend, arecv, gs, us, outs, held, held32,
    in_sem, x_send, x_recv, b_send, b_recv, a_send, a_recv,
    ga_send, ga_recv, gb_send, gb_recv, gx_send, gx_recv,
):
    f = lax.axis_index("fout")
    x, z = f // NZ, lax.rem(f, NZ)
    group, cls = z // 4, lax.rem(z, 4)

    def at(dx, dz):
        return {"fout": lax.rem(x + dx + NX, NX) * NZ + lax.rem(z + dz + NZ, NZ)}

    def copy(src, dst, send, recv, device):
        return pltpu.make_async_remote_copy(
            src_ref=src, dst_ref=dst, send_sem=send, recv_sem=recv,
            device_id=device, device_id_type=MESH,
        )

    def signal(sem, device):
        pl.semaphore_signal(sem, inc=1, device_id=device, device_id_type=MESH)

    def beside(k):
        return at(0, lax.rem(cls + k, 4) - cls)

    barrier = pltpu.get_barrier_semaphore()
    for d in (1, 2, 3):
        signal(barrier, beside(d))
    for d in (1, 2, 3):
        signal(barrier, at(d, 0))
    for m in range(1, GROUPS):
        @pl.when(group + m < GROUPS)
        def _():
            signal(barrier, at(0, 4 * m))

    fetch = [
        pltpu.make_async_copy(src, dst, in_sem.at[i])
        for i, (src, dst) in enumerate(((w_hbm, w_ref), (og_hbm, og_ref), (g_hbm, g_ref), (u_hbm, u_ref)))
    ]
    for c in fetch:
        c.start()

    row = lax.broadcasted_iota(jnp.int32, (TOK, TOK), 0)
    token = (
        32 * lax.rem(row // 32 + x, NX)
        + 16 * lax.rem(row // 16, 2)
        + lax.rem(lax.rem(row // 4, 4) + cls, 4)
        + 4 * lax.rem(row, 4)
    )
    pick = (lax.broadcasted_iota(jnp.int32, (TOK, TOK), 1) == token).astype(F32).astype(BF16)

    gs[...] = jnp.zeros_like(gs)
    us[...] = jnp.zeros_like(us)
    fetch[2].wait()
    fetch[3].wait()
    for c in range(CHUNKS):
        cols = slice(c * LANES, (c + 1) * LANES)
        gs[c : c + 1, :] = g_ref[:, cols].astype(F32)
        us[c : c + 1, :] = u_ref[:, cols].astype(F32)
    gate, up = gs[...], us[...]
    logistic = 1.0 / (1.0 + jnp.exp(-gate))
    activated = gate * logistic
    mine = pl.multiple_of(group * ROWS + (group // 4) * (12 * ROWS), ROWS)
    held[pl.ds(mine, ROWS), :] = (activated * up).astype(BF16)

    fetch[1].wait()
    ogp[...] = jnp.dot(pick, og_ref[...], preferred_element_type=F32).astype(BF16)

    fetch[0].wait()
    for c in range(CHUNKS):
        cols = slice(c * LANES, (c + 1) * LANES)
        product = lax.dot_general(
            ogp[...], w_ref[cols, :], (((1,), (1,)), ((), ())), preferred_element_type=F32
        )
        part[:, cols] = product[0:32, :]
        psend[:, cols] = product[32:, :].astype(BF16)

    pl.semaphore_wait(barrier, 6 + group)

    def x_copy(d, h):
        rows = pl.ds((d - 1) * 32 + h * HALF, HALF)
        return copy(psend.at[rows], xrecv.at[rows], x_send.at[h], x_recv.at[h], at(d, 0))

    def b_copy(h, k):
        rows = pl.ds(slot(0, h, k), 4 * ROWS)
        return copy(zsend.at[rows], brecv.at[rows], b_send.at[h], b_recv.at[h], beside(k))

    def a_copy(h, j):
        src = asend.at[pl.ds((h * 4 + j) * ROWS, ROWS)]
        dst = arecv.at[pl.ds(pl.multiple_of(group * ROWS, ROWS), ROWS)]
        target = {"fout": x * NZ + 16 * h + 4 * j + cls}
        return copy(src, dst, a_send.at[0], a_recv.at[0], target)

    def ga_copy(j):
        rows = pl.ds(mine, ROWS)
        target = {"fout": x * NZ + 4 * j + cls}
        return copy(held.at[rows], held.at[rows], ga_send.at[0], ga_recv.at[group], target)

    def ga_wait(j):
        rows = pl.ds(slot(0, j // 4, 0, j % 4), ROWS)
        return copy(held.at[rows], held.at[rows], ga_send.at[0], ga_recv.at[j], at(1, 0))

    def gb_copy(h, k):
        src, dst = pl.ds(slot(0, h, 0), 4 * ROWS), pl.ds(slot(0, h, k), 4 * ROWS)
        return copy(held.at[src], held.at[dst], gb_send.at[h], gb_recv.at[h], beside(4 - k))

    def gx_copy(b, h, others):
        first, rows = (1, 12 * ROWS) if others else (0, 4 * ROWS)
        src, dst = pl.ds(slot(0, h, first), rows), pl.ds(slot(b, h, first), rows)
        return copy(held.at[src], held.at[dst], gx_send.at[0], gx_recv.at[h, others], at(-b, 0))

    def arrived(ref, rows, sem):
        whole = ref.at[pl.ds(0, rows)]
        copy(whole, whole, sem, sem, at(1, 0)).wait_recv()

    def left(ref, rows, sem):
        whole = ref.at[pl.ds(0, rows)]
        copy(whole, whole, sem, sem, at(1, 0)).wait_send()

    def unpack(b, h, k):
        rows = pl.ds(slot(b, h, k), 4 * ROWS)
        held32[rows, :] = held[rows, :].astype(F32)

    def sum_x(h):
        arrived(xrecv, 3 * HALF, x_recv.at[h])
        for c in range(CHUNKS):
            cols = slice(c * LANES, (c + 1) * LANES)
            total = part[h * HALF : (h + 1) * HALF, cols]
            for d in (1, 2, 3):
                start = (d - 1) * 32 + h * HALF
                total += xrecv[start : start + HALF, cols].astype(F32)
            spread[pl.ds(h * HALF * ROWS + c, HALF, stride=ROWS), :] = total
        rows = pl.ds(slot(0, h, 1), 12 * ROWS)
        zsend[rows, :] = spread[rows, :].astype(BF16)
        for k in (2, 1, 3):
            b_copy(h, k).start()

    def sum_b(h):
        arrived(brecv, 12 * ROWS, b_recv.at[h])
        total = spread[pl.ds(slot(0, h, 0), 4 * ROWS), :]
        for k in (1, 2, 3):
            total += brecv[pl.ds(slot(0, h, k), 4 * ROWS), :].astype(F32)
        asend[pl.ds(h * 4 * ROWS, 4 * ROWS), :] = total.astype(BF16)
        for j in range(4):
            @pl.when(group > h * 4 + j)
            def _():
                a_copy(h, j).start()

            @pl.when(group == h * 4 + j)
            def _():
                arecv[pl.ds((h * 4 + j) * ROWS, ROWS), :] = asend[pl.ds((h * 4 + j) * ROWS, ROWS), :]

    def answer_row(j):
        @pl.when(group < j)
        def _():
            ga_wait(j).wait_recv()
            ga_copy(j).start()

    def answer_sum(j):
        @pl.when(group < j)
        def _():
            a_copy(j // 4, j % 4).start()

    def below(h, end=4, start=0):
        for j in range(4 * h + start, 4 * h + end):
            @pl.when(group > j)
            def _():
                ga_wait(j).wait_recv()

    def gather(h):
        gather_start(h)
        gather_end(h)

    def gather_start(h):
        for k in (2, 1, 3):
            gb_copy(h, k).start()
        for b in (2, 1, 3):
            gx_copy(b, h, 0).start()
        unpack(0, h, 0)

    def gather_end(h):
        arrived(held, 12 * ROWS, gb_recv.at[h])
        for b in (2, 1, 3):
            gx_copy(b, h, 1).start()
        for k in (1, 2, 3):
            unpack(0, h, k)

    def finish_sums():
        arrived(arecv, 7 * ROWS, a_recv.at[0])
        upstream = arecv[0:ROWS, :].astype(F32)
        for j in range(1, 8):
            upstream += arecv[j * ROWS : (j + 1) * ROWS, :].astype(F32)
        gate, up = gs[...], us[...]
        logistic = 1.0 / (1.0 + jnp.exp(-gate))
        outs[0:ROWS, :] = upstream * up * logistic * (1.0 + gate * (1.0 - logistic))
        outs[ROWS:, :] = upstream * (gate * logistic)
        for c in range(CHUNKS):
            cols = slice(c * LANES, (c + 1) * LANES)
            gg_ref[:, cols] = outs[c : c + 1, :].astype(BF16)
            ug_ref[:, cols] = outs[ROWS + c : ROWS + c + 1, :].astype(BF16)

    for j in range(GROUPS - 1):
        @pl.when(group > j)
        def _():
            ga_copy(j).start()
    for d in (2, 1, 3):
        x_copy(d, 0).start()
    left(psend, 3 * HALF, x_send.at[0])
    for d in (2, 1, 3):
        x_copy(d, 1).start()
    sum_x(0)
    sum_b(0)

    @pl.when(group == 3)
    def _():
        answer_row(4)
        answer_row(5)

    @pl.when(group >= 4)
    def _():
        answer_row(5)

    sum_x(1)

    @pl.when(group >= 3)
    def _():
        answer_row(6)

    sum_b(1)

    @pl.when(group < 3)
    def _():
        for j in (1, 2, 3):
            answer_row(j)
            answer_sum(j)
        below(0)
        gather(0)
        for j in (5, 6, 7, 4):
            answer_row(j)
        gather_start(1)
        for j in (7, 6, 5, 4):
            answer_sum(j)
        gather_end(1)

    @pl.when(group >= 3)
    def _():
        answer_row(7)
        for j in (7, 6, 5, 4):
            answer_sum(j)
        below(1)
        gather_start(1)
        below(0, 2)
        gather_end(1)
        below(0, 4, 2)
        gather_start(0)
        gather_end(0)

    finish_sums()
    for h in (0, 1):
        for others in (0, 1):
            arrived(held, (36 if others else 12) * ROWS, gx_recv.at[h, others])
            for b in (1, 2, 3):
                for k in (1, 2, 3) if others else (0,):
                    unpack(b, h, k)

    for c in range(CHUNKS):
        hidden = held32[pl.ds(c, TOK, stride=ROWS), :].astype(BF16)
        grad = lax.dot_general(
            hidden, ogp[...], (((0,), (0,)), ((), ())), preferred_element_type=F32
        )
        dg_ref[c * LANES : (c + 1) * LANES, :] = grad.astype(BF16)

    left(psend, 3 * HALF, x_send.at[1])
    for h in (0, 1):
        left(zsend, 12 * ROWS, b_send.at[h])
        left(held, 12 * ROWS, gb_send.at[h])
    left(asend, 7 * ROWS, a_send.at[0])
    left(held, 7 * ROWS, ga_send.at[0])
    left(held, 96 * ROWS, gx_send.at[0])


def local(gate_pre, up_pre, out_grad, down_weight):
    dma = pltpu.SemaphoreType.DMA
    vmem = pl.BlockSpec(memory_space=pltpu.VMEM)
    shapes = (
        jax.ShapeDtypeStruct((1, UNITS), BF16),
        jax.ShapeDtypeStruct((1, UNITS), BF16),
        jax.ShapeDtypeStruct((UNITS, LANES), BF16),
    )
    anywhere = pl.BlockSpec(memory_space=pl.ANY)
    operands = [
        pltpu.with_memory_space_constraint(a, pltpu.HBM)
        for a in (gate_pre, up_pre, out_grad, down_weight)
    ]
    return pl.pallas_call(
        kernel,
        out_shape=shapes,
        in_specs=[anywhere] * 4,
        out_specs=(vmem,) * 3,
        scratch_shapes=[
            pltpu.VMEM((1, UNITS), BF16),
            pltpu.VMEM((1, UNITS), BF16),
            pltpu.VMEM((TOK, LANES), BF16),
            pltpu.VMEM((UNITS, LANES), BF16),
            pltpu.VMEM((TOK, LANES), BF16),
            pltpu.VMEM((32, UNITS), F32),
            pltpu.VMEM((96, UNITS), BF16),
            pltpu.VMEM((96, UNITS), BF16),
            pltpu.VMEM((32 * ROWS, LANES), F32),
            pltpu.VMEM((32 * ROWS, LANES), BF16),
            pltpu.VMEM((32 * ROWS, LANES), BF16),
            pltpu.VMEM((8 * ROWS, LANES), BF16),
            pltpu.VMEM((8 * ROWS, LANES), BF16),
            pltpu.VMEM((ROWS, LANES), F32),
            pltpu.VMEM((ROWS, LANES), F32),
            pltpu.VMEM((2 * ROWS, LANES), F32),
            pltpu.VMEM((TOK * ROWS, LANES), BF16),
            pltpu.VMEM((TOK * ROWS, LANES), F32),
            dma((4,)),
            dma((2,)), dma((2,)),
            dma((2,)), dma((2,)),
            dma((1,)), dma((1,)),
            dma((1,)), dma((8,)),
            dma((2,)), dma((2,)),
            dma((1,)), dma((2, 2)),
        ],
        compiler_params=pltpu.CompilerParams(
            collective_id=0, has_side_effects=True, vmem_limit_bytes=32 * 2**20
        ),
    )(*operands)


def solution(mesh):
    placed = (P("fout", "fin"), P("fout", "fin"), P(None, "fout"), P("fin", "fout"))
    return jax.shard_map(
        local,
        mesh=mesh,
        in_specs=placed,
        out_specs=(P("fout", "fin"), P("fout", "fin"), P("fin", "fout")),
        check_vma=False,
    )
```

```python
import jax
import jax.numpy as jnp
from jax import lax
from jax.experimental import pallas as pl
from jax.experimental.pallas import tpu as pltpu
from jax.sharding import PartitionSpec as P

MESH = pl.DeviceIdType.MESH
F32, BF16 = jnp.float32, jnp.bfloat16
NX, NZ = 4, 32
TOK = 128
UNITS = 3456
LANES = 128
CHUNKS = UNITS // LANES
ROWS = 32
HALF = 16
GROUPS = NZ // 4


def slot(b, h, k, j=0):
    return (((b * 2 + h) * 4 + k) * 4 + j) * ROWS


def kernel(
    g_hbm, u_hbm, og_hbm, w_hbm, gg_ref, ug_ref, dg_ref,
    g_ref, u_ref, og_ref, w_ref,
    ogp, part, psend, xrecv, spread, zsend, brecv, asend, arecv, gs, us, outs, held, held32,
    in_sem, x_send, x_recv, b_send, b_recv, a_send, a_recv,
    ga_send, ga_recv, gb_send, gb_recv, gx_send, gx_recv,
):
    f = lax.axis_index("fout")
    x, z = f // NZ, lax.rem(f, NZ)
    group, cls = z // 4, lax.rem(z, 4)

    def at(dx, dz):
        return {"fout": lax.rem(x + dx + NX, NX) * NZ + lax.rem(z + dz + NZ, NZ)}

    def copy(src, dst, send, recv, device):
        return pltpu.make_async_remote_copy(
            src_ref=src, dst_ref=dst, send_sem=send, recv_sem=recv,
            device_id=device, device_id_type=MESH,
        )

    def signal(sem, device):
        pl.semaphore_signal(sem, inc=1, device_id=device, device_id_type=MESH)

    def beside(k):
        return at(0, lax.rem(cls + k, 4) - cls)

    barrier = pltpu.get_barrier_semaphore()
    for d in (1, 2, 3):
        signal(barrier, beside(d))
    for d in (1, 2, 3):
        signal(barrier, at(d, 0))
    for m in range(1, GROUPS):
        @pl.when(group + m < GROUPS)
        def _():
            signal(barrier, at(0, 4 * m))

    fetch = [
        pltpu.make_async_copy(src, dst, in_sem.at[i])
        for i, (src, dst) in enumerate(((w_hbm, w_ref), (og_hbm, og_ref), (g_hbm, g_ref), (u_hbm, u_ref)))
    ]
    for c in fetch:
        c.start()

    row = lax.broadcasted_iota(jnp.int32, (TOK, TOK), 0)
    token = (
        32 * lax.rem(row // 32 + x, NX)
        + 16 * lax.rem(row // 16, 2)
        + lax.rem(lax.rem(row // 4, 4) + cls, 4)
        + 4 * lax.rem(row, 4)
    )
    pick = (lax.broadcasted_iota(jnp.int32, (TOK, TOK), 1) == token).astype(F32).astype(BF16)

    gs[...] = jnp.zeros_like(gs)
    us[...] = jnp.zeros_like(us)
    fetch[2].wait()
    fetch[3].wait()
    for c in range(CHUNKS):
        cols = slice(c * LANES, (c + 1) * LANES)
        gs[c : c + 1, :] = g_ref[:, cols].astype(F32)
        us[c : c + 1, :] = u_ref[:, cols].astype(F32)
    gate, up = gs[...], us[...]
    logistic = 1.0 / (1.0 + jnp.exp(-gate))
    activated = gate * logistic
    mine = pl.multiple_of(group * ROWS + (group // 4) * (12 * ROWS), ROWS)
    held[pl.ds(mine, ROWS), :] = (activated * up).astype(BF16)

    fetch[1].wait()
    ogp[...] = jnp.dot(pick, og_ref[...], preferred_element_type=F32).astype(BF16)

    fetch[0].wait()
    for c in range(CHUNKS):
        cols = slice(c * LANES, (c + 1) * LANES)
        product = lax.dot_general(
            ogp[...], w_ref[cols, :], (((1,), (1,)), ((), ())), preferred_element_type=F32
        )
        part[:, cols] = product[0:32, :]
        psend[:, cols] = product[32:, :].astype(BF16)

    pl.semaphore_wait(barrier, 6 + group)

    def x_copy(d, h):
        rows = pl.ds((d - 1) * 32 + h * HALF, HALF)
        return copy(psend.at[rows], xrecv.at[rows], x_send.at[h], x_recv.at[h], at(d, 0))

    def b_copy(h, k):
        rows = pl.ds(slot(0, h, k), 4 * ROWS)
        return copy(zsend.at[rows], brecv.at[rows], b_send.at[h], b_recv.at[h], beside(k))

    def a_copy(h, j):
        src = asend.at[pl.ds((h * 4 + j) * ROWS, ROWS)]
        dst = arecv.at[pl.ds(pl.multiple_of(group * ROWS, ROWS), ROWS)]
        target = {"fout": x * NZ + 16 * h + 4 * j + cls}
        return copy(src, dst, a_send.at[0], a_recv.at[0], target)

    def ga_copy(j):
        rows = pl.ds(mine, ROWS)
        target = {"fout": x * NZ + 4 * j + cls}
        return copy(held.at[rows], held.at[rows], ga_send.at[0], ga_recv.at[group], target)

    def ga_wait(j):
        rows = pl.ds(slot(0, j // 4, 0, j % 4), ROWS)
        return copy(held.at[rows], held.at[rows], ga_send.at[0], ga_recv.at[j], at(1, 0))

    def gb_copy(h, k):
        src, dst = pl.ds(slot(0, h, 0), 4 * ROWS), pl.ds(slot(0, h, k), 4 * ROWS)
        return copy(held.at[src], held.at[dst], gb_send.at[h], gb_recv.at[h], beside(4 - k))

    def gx_copy(b, h, others):
        first, rows = (1, 12 * ROWS) if others else (0, 4 * ROWS)
        src, dst = pl.ds(slot(0, h, first), rows), pl.ds(slot(b, h, first), rows)
        return copy(held.at[src], held.at[dst], gx_send.at[0], gx_recv.at[h, others], at(-b, 0))

    def arrived(ref, rows, sem):
        whole = ref.at[pl.ds(0, rows)]
        copy(whole, whole, sem, sem, at(1, 0)).wait_recv()

    def left(ref, rows, sem):
        whole = ref.at[pl.ds(0, rows)]
        copy(whole, whole, sem, sem, at(1, 0)).wait_send()

    def unpack(b, h, k):
        rows = pl.ds(slot(b, h, k), 4 * ROWS)
        held32[rows, :] = held[rows, :].astype(F32)

    def sum_x(h):
        arrived(xrecv, 3 * HALF, x_recv.at[h])
        for c in range(CHUNKS):
            cols = slice(c * LANES, (c + 1) * LANES)
            total = part[h * HALF : (h + 1) * HALF, cols]
            for d in (1, 2, 3):
                start = (d - 1) * 32 + h * HALF
                total += xrecv[start : start + HALF, cols].astype(F32)
            spread[pl.ds(h * HALF * ROWS + c, HALF, stride=ROWS), :] = total
        rows = pl.ds(slot(0, h, 1), 12 * ROWS)
        zsend[rows, :] = spread[rows, :].astype(BF16)
        for k in (2, 1, 3):
            b_copy(h, k).start()

    def sum_b(h):
        arrived(brecv, 12 * ROWS, b_recv.at[h])
        total = spread[pl.ds(slot(0, h, 0), 4 * ROWS), :]
        for k in (1, 2, 3):
            total += brecv[pl.ds(slot(0, h, k), 4 * ROWS), :].astype(F32)
        asend[pl.ds(h * 4 * ROWS, 4 * ROWS), :] = total.astype(BF16)
        for j in range(4):
            @pl.when(group > h * 4 + j)
            def _():
                a_copy(h, j).start()

            @pl.when(group == h * 4 + j)
            def _():
                arecv[pl.ds((h * 4 + j) * ROWS, ROWS), :] = asend[pl.ds((h * 4 + j) * ROWS, ROWS), :]

    def answer_row(j):
        @pl.when(group < j)
        def _():
            ga_wait(j).wait_recv()
            ga_copy(j).start()

    def answer_sum(j):
        @pl.when(group < j)
        def _():
            a_copy(j // 4, j % 4).start()

    def below(h, end=4, start=0):
        for j in range(4 * h + start, 4 * h + end):
            @pl.when(group > j)
            def _():
                ga_wait(j).wait_recv()

    def gather(h):
        gather_start(h)
        gather_end(h)

    def gather_start(h):
        for k in (2, 1, 3):
            gb_copy(h, k).start()
        for b in (2, 1, 3):
            gx_copy(b, h, 0).start()
        unpack(0, h, 0)

    def gather_end(h):
        arrived(held, 12 * ROWS, gb_recv.at[h])
        for b in (2, 1, 3):
            gx_copy(b, h, 1).start()
        for k in (1, 2, 3):
            unpack(0, h, k)

    def finish_sums():
        arrived(arecv, 7 * ROWS, a_recv.at[0])
        upstream = arecv[0:ROWS, :].astype(F32)
        for j in range(1, 8):
            upstream += arecv[j * ROWS : (j + 1) * ROWS, :].astype(F32)
        gate, up = gs[...], us[...]
        logistic = 1.0 / (1.0 + jnp.exp(-gate))
        outs[0:ROWS, :] = upstream * up * logistic * (1.0 + gate * (1.0 - logistic))
        outs[ROWS:, :] = upstream * (gate * logistic)
        for c in range(CHUNKS):
            cols = slice(c * LANES, (c + 1) * LANES)
            gg_ref[:, cols] = outs[c : c + 1, :].astype(BF16)
            ug_ref[:, cols] = outs[ROWS + c : ROWS + c + 1, :].astype(BF16)

    for j in range(GROUPS - 1):
        @pl.when(group > j)
        def _():
            ga_copy(j).start()
    for d in (2, 1, 3):
        x_copy(d, 0).start()
    left(psend, 3 * HALF, x_send.at[0])
    for d in (2, 1, 3):
        x_copy(d, 1).start()
    sum_x(0)
    sum_b(0)

    @pl.when(group == 3)
    def _():
        answer_row(4)
        answer_row(5)

    @pl.when(group >= 4)
    def _():
        answer_row(5)

    sum_x(1)

    @pl.when(group >= 3)
    def _():
        answer_row(6)

    sum_b(1)

    @pl.when(group < 3)
    def _():
        for j in (1, 2, 3):
            answer_row(j)
            answer_sum(j)
        below(0)
        gather(0)
        for j in (5, 6, 7, 4):
            answer_row(j)
        gather_start(1)
        for j in (7, 6, 5, 4):
            answer_sum(j)
        gather_end(1)

    @pl.when(group >= 3)
    def _():
        answer_row(7)
        for j in (7, 6, 5, 4):
            answer_sum(j)
        below(1)
        gather_start(1)
        below(0, 2)
        gather_end(1)
        below(0, 4, 2)
        gather_start(0)
        gather_end(0)

    finish_sums()
    for h in (0, 1):
        for others in (0, 1):
            arrived(held, (36 if others else 12) * ROWS, gx_recv.at[h, others])
            for b in (1, 2, 3):
                for k in (1, 2, 3) if others else (0,):
                    unpack(b, h, k)

    for c in range(CHUNKS):
        hidden = held32[pl.ds(c, TOK, stride=ROWS), :].astype(BF16)
        grad = lax.dot_general(
            hidden, ogp[...], (((0,), (0,)), ((), ())), preferred_element_type=F32
        )
        dg_ref[c * LANES : (c + 1) * LANES, :] = grad.astype(BF16)

    left(psend, 3 * HALF, x_send.at[1])
    for h in (0, 1):
        left(zsend, 12 * ROWS, b_send.at[h])
        left(held, 12 * ROWS, gb_send.at[h])
    left(asend, 7 * ROWS, a_send.at[0])
    left(held, 7 * ROWS, ga_send.at[0])
    left(held, 96 * ROWS, gx_send.at[0])


def local(gate_pre, up_pre, out_grad, down_weight):
    dma = pltpu.SemaphoreType.DMA
    vmem = pl.BlockSpec(memory_space=pltpu.VMEM)
    shapes = (
        jax.ShapeDtypeStruct((1, UNITS), BF16),
        jax.ShapeDtypeStruct((1, UNITS), BF16),
        jax.ShapeDtypeStruct((UNITS, LANES), BF16),
    )
    anywhere = pl.BlockSpec(memory_space=pl.ANY)
    operands = [
        pltpu.with_memory_space_constraint(a, pltpu.HBM)
        for a in (gate_pre, up_pre, out_grad, down_weight)
    ]
    return pl.pallas_call(
        kernel,
        out_shape=shapes,
        in_specs=[anywhere] * 4,
        out_specs=(vmem,) * 3,
        scratch_shapes=[
            pltpu.VMEM((1, UNITS), BF16),
            pltpu.VMEM((1, UNITS), BF16),
            pltpu.VMEM((TOK, LANES), BF16),
            pltpu.VMEM((UNITS, LANES), BF16),
            pltpu.VMEM((TOK, LANES), BF16),
            pltpu.VMEM((32, UNITS), F32),
            pltpu.VMEM((96, UNITS), BF16),
            pltpu.VMEM((96, UNITS), BF16),
            pltpu.VMEM((33 * ROWS, LANES), F32),
            pltpu.VMEM((32 * ROWS, LANES), BF16),
            pltpu.VMEM((32 * ROWS, LANES), BF16),
            pltpu.VMEM((8 * ROWS, LANES), BF16),
            pltpu.VMEM((8 * ROWS, LANES), BF16),
            pltpu.VMEM((ROWS, LANES), F32),
            pltpu.VMEM((ROWS, LANES), F32),
            pltpu.VMEM((2 * ROWS, LANES), F32),
            pltpu.VMEM((TOK * ROWS, LANES), BF16),
            pltpu.VMEM((TOK * ROWS + ROWS, LANES), F32),
            dma((4,)),
            dma((2,)), dma((2,)),
            dma((2,)), dma((2,)),
            dma((1,)), dma((1,)),
            dma((1,)), dma((8,)),
            dma((2,)), dma((2,)),
            dma((1,)), dma((2, 2)),
        ],
        compiler_params=pltpu.CompilerParams(
            collective_id=0, has_side_effects=True, vmem_limit_bytes=32 * 2**20
        ),
    )(*operands)


def solution(mesh):
    placed = (P("fout", "fin"), P("fout", "fin"), P(None, "fout"), P("fin", "fout"))
    return jax.shard_map(
        local,
        mesh=mesh,
        in_specs=placed,
        out_specs=(P("fout", "fin"), P("fout", "fin"), P("fin", "fout")),
        check_vma=False,
    )
```
